32 devices in a mesh: groups: 2 (over y), loop: 4 (over z), band: 2 (over x), win: 2 (over core).
Axes of the slice: x: 2, y: 2, z: 4, core: 2. Of those that a mesh axis runs over, the one named last changes fastest.
Arguments:
- spectra_phase: bfloat16 [8, 512, 1280], P(('groups', 'win'), 'band', 'loop'), parts along dimension 0, may hold values from -3.140625 to 3.140625
- window_valid: int32 [8, 1280], P('groups', 'loop'), parts along dimension 0, may hold values 0 or 1
- band_gain: float32 [512], P('band'), may hold values from 0.02 to 0.2
- cross_index: int32 [2560, 8], P(('groups', 'loop')), parts along dimension 0, may hold values from 0 to 319
Outputs:
- coherence: float32 [2560, 2, 320], P(('groups', 'loop', 'band', 'win')), parts along dimension 0
- crossing: float32 [2560, 8], P(('groups', 'loop', 'band', 'win')), parts along dimension 0
The draws below stay inside these ranges and needn't reach their ends.
There are 2 independent parts, one for each index of `groups`. The reference program is written for one: setup_inputs(seed, part) draws one part's arguments, and reference() takes and returns one part's arrays. A program takes and returns all parts, laid end to end along the dimension named above; an argument that names none is the same for every part. Nothing has to cross between parts.
Inputs may be any that keep to these rules, and one draw needn't show every extreme that they name: `window_valid`: 1 marks a usable window of a channel, 0 a rejected one. `cross_index`: each entry is a channel position within the opposite block.
All inputs are finite; a program needn't handle non-finite values. No bound on the sum of `window_valid` on one device may be relied on, other than what follows from the above.
Results may differ from the reference program's by a relative error of at most 0.0037.
Values may be sent and summed in bfloat16 or wider, within the bound.
A program may use at most 64 MiB of HBM per device.

```python
import math
import jax
import jax.numpy as jnp
from jax import lax

CB = 320
WIN = 4
FREQ = 512
NEAR = 8
CHANNELS = 1280
N_LOOP = 4


def place_ends(entries, own_key, least, top_value):
    extent = entries.shape
    spot = [jax.random.randint(jax.random.fold_in(own_key, axis), (), 0, extent[axis]) for axis in range(len(extent))]
    entries = entries.at[tuple(spot)].set(least)
    longest = extent.index(max(extent))
    spot[longest] = (spot[longest] + 1) % extent[longest]
    return entries.at[tuple(spot)].set(top_value)


def steps_of(key, extent, shards, low, high):
    gain = 1.0
    for dim, parts in shards:
        draws = jax.random.uniform(jax.random.fold_in(jax.random.fold_in(key, 6), dim), (parts,), jnp.float32, low / len(shards), high / len(shards))
        gain = gain * jnp.repeat(jnp.exp(draws), extent[dim] // parts).reshape((-1,) + (1,) * (len(extent) - 1 - dim))
    return gain


def setup_inputs(seed: int = 0, part: int = 0) -> dict:
    seeds = jax.random.split(jax.random.key(seed), 5)
    own_keys = jax.random.split(jax.random.fold_in(seeds[4], part), 5)
    spectra_phase = jnp.clip(jax.random.uniform(own_keys[0], (WIN, FREQ, CHANNELS), jnp.float32, -3.140625, 3.140625), -3.140625, 3.140625).astype(jnp.bfloat16)
    window_valid = place_ends((jax.random.randint(own_keys[1], (WIN, CHANNELS), 0, 4) < 3).astype(jnp.int32), jax.random.fold_in(own_keys[1], 1), 0, 1)
    band_gain = jnp.clip(jnp.exp(math.log(0.2) - 2.3025851 * jax.random.uniform(seeds[2], (FREQ,), jnp.float32) ** steps_of(seeds[2], (FREQ,), ((0, 2),), -0.2, 0.2)), 0.02, 0.2)
    cross_index = place_ends(jax.random.randint(own_keys[3], (CHANNELS, NEAR), 0, CB), jax.random.fold_in(own_keys[3], 1), 0, CB - 1).astype(jnp.int32)
    return dict(spectra_phase=spectra_phase, window_valid=window_valid, band_gain=band_gain, cross_index=cross_index)


def trig_sides(spectra_phase, window_valid, band_gain):
    phases = spectra_phase.astype(jnp.float32)
    valid_rows = window_valid.astype(jnp.float32)[:, None, :]
    weights = band_gain.astype(jnp.float32)[None, :, None]
    cosine = jnp.cos(phases)
    sine = jnp.sin(phases)
    own_side = jnp.stack([cosine * weights * valid_rows, sine * weights * valid_rows]).astype(jnp.bfloat16)
    far_side = jnp.stack([cosine * valid_rows, sine * valid_rows]).astype(jnp.bfloat16)
    channel_total = phases.shape[-1]
    return own_side.reshape(-1, channel_total), far_side.reshape(-1, channel_total)


def reference(spectra_phase, window_valid, band_gain, cross_index):
    own_side, far_side = trig_sides(spectra_phase, window_valid, band_gain)
    valid_flags = window_valid.astype(jnp.float32)
    offset_count = N_LOOP // 4 + 1

    def one_block(block_index):
        own_part = lax.dynamic_slice_in_dim(own_side, block_index * CB, CB, 1)
        own_flags = lax.dynamic_slice_in_dim(valid_flags, block_index * CB, CB, 1)

        def pair_ratio(partner):
            first_col = (partner * CB).astype(jnp.int32)
            far_part = lax.dynamic_slice_in_dim(far_side, first_col, CB, 1)
            far_flags = lax.dynamic_slice_in_dim(valid_flags, first_col, CB, 1)
            numerator = jnp.dot(own_part.T, far_part, preferred_element_type=jnp.float32)
            counts = jnp.dot(own_flags.T, far_flags, precision=lax.Precision.HIGHEST)
            return numerator / jnp.maximum(counts, 1.0)

        cycle_terms = jnp.concatenate([pair_ratio((block_index + offset) % N_LOOP) for offset in range(offset_count)], axis=1)
        crossed = pair_ratio((block_index + N_LOOP // 2) % N_LOOP)
        chosen = lax.dynamic_slice_in_dim(cross_index, block_index * CB, CB, 0)
        return cycle_terms, jnp.take_along_axis(crossed, chosen, axis=1)

    cycle_terms, crossed = lax.map(one_block, jnp.arange(N_LOOP, dtype=jnp.int32))
    return cycle_terms.reshape(N_LOOP * CB, offset_count, CB), crossed.reshape(N_LOOP * CB, NEAR)
```

```python
import functools
import math

import jax
import jax.numpy as jnp
from jax import lax
from jax.experimental import pallas as pl
from jax.experimental.pallas import tpu as pltpu
from jax.sharding import PartitionSpec as P

MESH = pl.DeviceIdType.MESH
SIN = (0.9999995827674866, -0.16666549444198608, 0.008332383818924427,
       -0.00019808131037279963, 2.6991506274498533e-06, -2.033945278867577e-08)
COS = (1.0, -0.49999988079071045, 0.041666485369205475, -0.0013887780951336026,
       2.4769393348833546e-05, -2.707419355374441e-07, 1.7227314019763185e-09)
FLAG_ROWS = 8


def horner(coefficients, u):
    total = coefficients[-1] * u + coefficients[-2]
    for c in coefficients[-3::-1]:
        total = total * u + c
    return total


def cos_sin(x):
    u = x * x
    return horner(COS, u), horner(SIN, u) * x


def dot_t(a, b):
    return lax.dot_general(a, b, (((1,), (1,)), ((), ())), preferred_element_type=jnp.float32)


def row_dot(a, b):
    return lax.dot_general(a, b, (((1,), (0,)), ((), ())), preferred_element_type=jnp.float32)


def kernel(
    plan, phase_ref, valid_ref, gain_ref, index_ref, coh_ref, cross_ref,
    phase, far_phase, own_flags, far_flags, turn, columns, own_side, far_side,
    part, part_in, xpart, xpart_in,
    load_sem, flag_send, flag_recv, loop_send, loop_recv, sum_send, sum_recv,
):
    n_loop, n_band, n_win, offsets, chunk = plan
    wins, channels, freq = phase.shape
    cycles = part.shape[0]
    owners = n_band * n_win
    own_rows = channels // owners
    windows = valid_ref.shape[0]
    far_slots = len(offsets)
    loop_at = lax.axis_index("loop")
    win_at = lax.axis_index("win")
    owner_at = lax.axis_index("band") * n_win + win_at

    def loop_device(steps):
        return {"loop": lax.rem(loop_at + (steps % n_loop), n_loop)}

    def owner_of(d):
        return lax.rem(owner_at + d, owners)

    def owner_device(d):
        owner = owner_of(d)
        return {"band": owner // n_win, "win": lax.rem(owner, n_win)}

    barrier = pltpu.get_barrier_semaphore()
    greeted = sorted({o % n_loop for o in offsets} | {-o % n_loop for o in offsets})
    for steps in greeted:
        pl.semaphore_signal(barrier, inc=1, device_id=loop_device(steps), device_id_type=MESH)
    for d in range(1, owners):
        pl.semaphore_signal(barrier, inc=1, device_id=owner_device(d), device_id_type=MESH)
    loads = [
        pltpu.make_async_copy(phase_ref.at[w], phase.at[w], load_sem.at[w]) for w in range(wins)
    ]
    for load in loads:
        load.start()
    own_flags[...] = jnp.zeros_like(own_flags)
    own_flags[0:windows, :] = valid_ref[...].astype(jnp.float32)
    pl.semaphore_wait(barrier, len(greeted) + owners - 1)

    flag_copies, loop_copies = [], []
    for p, offset in enumerate(offsets):
        copy = pltpu.make_async_remote_copy(
            own_flags, far_flags.at[p], flag_send.at[p], flag_recv.at[p],
            device_id=loop_device(-offset), device_id_type=MESH,
        )
        copy.start()
        flag_copies.append(copy)
    for p, offset in enumerate(offsets):
        copies = []
        for w in range(wins):
            copy = pltpu.make_async_remote_copy(
                phase_ref.at[w], far_phase.at[p, w], loop_send.at[p, w], loop_recv.at[p, w],
                device_id=loop_device(-offset), device_id_type=MESH,
            )
            copy.start()
            copies.append(copy)
        loop_copies.append(copies)

    def window_row(flags_ref, w):
        return flags_ref[pl.ds(win_at * wins + w, 1), :]

    def turned(flags_ref, slot):
        turn[...] = jnp.zeros_like(turn)
        turn[0:FLAG_ROWS, 0:channels] = flags_ref[...]
        for w in range(wins):
            turn[FLAG_ROWS + w : FLAG_ROWS + w + 1, 0:channels] = window_row(flags_ref, w)
        columns[slot] = jnp.transpose(turn[...])[0:channels, :]

    def column(slot, w):
        return columns[slot, :, FLAG_ROWS + w : FLAG_ROWS + w + 1]

    def inverse_counts(slot, flags_ref):
        counts = row_dot(columns[slot, :, 0:FLAG_ROWS], flags_ref[...])
        return 1.0 / jnp.maximum(counts, 1.0)

    def far_trig(source, w):
        def step(c, _):
            rows = pl.ds(pl.multiple_of(c * chunk, chunk), chunk)
            cosine, sine = cos_sin(source[rows, :].astype(jnp.float32))
            far_side[w, rows, 0:freq] = cosine.astype(jnp.bfloat16)
            far_side[w, rows, freq : 2 * freq] = sine.astype(jnp.bfloat16)
            return 0

        lax.fori_loop(0, channels // chunk, step, 0)

    turned(own_flags, 0)
    gain = gain_ref[...]

    def own_trig(w):
        def step(c, _):
            rows = pl.ds(pl.multiple_of(c * chunk, chunk), chunk)
            cosine, sine = cos_sin(phase[w, rows, :].astype(jnp.float32))
            far_side[w, rows, 0:freq] = cosine.astype(jnp.bfloat16)
            far_side[w, rows, freq : 2 * freq] = sine.astype(jnp.bfloat16)
            factor = gain * columns[0, rows, FLAG_ROWS + w : FLAG_ROWS + w + 1]
            own_side[w, rows, 0:freq] = (cosine * factor).astype(jnp.bfloat16)
            own_side[w, rows, freq : 2 * freq] = (sine * factor).astype(jnp.bfloat16)
            return 0

        lax.fori_loop(0, channels // chunk, step, 0)

    sums = []

    def send_sum(piece, source, target, d):
        copy = pltpu.make_async_remote_copy(
            source.at[owner_of(d)], target.at[d - 1],
            sum_send.at[piece, d - 1], sum_recv.at[piece, d - 1],
            device_id=owner_device(d), device_id_type=MESH,
        )
        copy.start()
        sums.append(copy)

    def coherence_piece(k, flags_ref):
        ratio = dot_t(own_side[0], far_side[0]) * window_row(flags_ref, 0)
        for w in range(1, wins):
            ratio += dot_t(own_side[w], far_side[w]) * window_row(flags_ref, w)
        ratio = ratio * inverse_counts(0, flags_ref)
        for r in range(owners):
            part[k, r] = ratio[r * own_rows : (r + 1) * own_rows, :].astype(jnp.bfloat16)
        for d in range(1, owners):
            send_sum(k, part.at[k], part_in.at[k], d)

    for w in range(wins):
        loads[w].wait()
        own_trig(w)
    coherence_piece(0, own_flags)

    for p in range(far_slots):
        flags_ref = far_flags.at[p]
        flag_copies[p].wait_recv()
        if p == far_slots - 1:
            turned(flags_ref, 1)
        for w in range(wins):
            loop_copies[p][w].wait_recv()
            far_trig(far_phase.at[p, w], w)
        if p < far_slots - 1:
            coherence_piece(p + 1, flags_ref)
        else:
            ratio = dot_t(far_side[0], own_side[0]) * column(1, 0)
            for w in range(1, wins):
                ratio += dot_t(far_side[w], own_side[w]) * column(1, w)
            ratio = ratio * inverse_counts(1, own_flags)
            position = lax.broadcasted_iota(jnp.int32, ratio.shape, 0)
            near = index_ref.shape[0]
            chosen = jnp.concatenate(
                [
                    jnp.sum(
                        jnp.where(position == index_ref[n : n + 1, :], ratio, 0.0),
                        axis=0, keepdims=True,
                    )
                    for n in range(near)
                ],
                axis=0,
            )
            for r in range(owners):
                xpart[r, :, 0:own_rows] = chosen[:, r * own_rows : (r + 1) * own_rows]
            for d in range(1, owners):
                send_sum(cycles, xpart, xpart_in, d)

    for k in range(cycles):
        total = part[k, owner_at].astype(jnp.float32)
        for d in range(1, owners):
            sums[k * (owners - 1) + d - 1].wait_recv()
            total += part_in[k, d - 1].astype(jnp.float32)
        coh_ref[:, k, :] = total
    total = xpart[owner_at]
    for d in range(1, owners):
        sums[cycles * (owners - 1) + d - 1].wait_recv()
        total += xpart_in[d - 1]
    cross_ref[...] = total[:, 0:own_rows]

    for copy in flag_copies:
        copy.wait_send()
    for copies in loop_copies:
        for copy in copies:
            copy.wait_send()
    for copy in sums:
        copy.wait_send()


def on_device(spectra_phase, window_valid, band_gain, cross_index):
    wins, freq, channels = spectra_phase.shape
    windows = window_valid.shape[0]
    near = cross_index.shape[1]
    n_loop = lax.axis_size("loop")
    n_band = lax.axis_size("band")
    n_win = lax.axis_size("win")
    owners = n_band * n_win
    own_rows = channels // owners
    far_reach = n_loop // 4
    offsets = tuple(range(1, far_reach + 1)) + (n_loop // 2,)
    cycles = far_reach + 1
    slots = len(offsets)
    chunk = math.gcd(channels, 32)
    lanes = -(-own_rows // 128) * 128
    wide = -(-channels // 128) * 128
    vmem = pl.BlockSpec(memory_space=pltpu.VMEM)
    coherence, crossing = pl.pallas_call(
        functools.partial(kernel, (n_loop, n_band, n_win, offsets, chunk)),
        out_shape=(
            jax.ShapeDtypeStruct((own_rows, cycles, channels), jnp.float32),
            jax.ShapeDtypeStruct((near, own_rows), jnp.float32),
        ),
        in_specs=[pl.BlockSpec(memory_space=pl.ANY), vmem, vmem, vmem],
        out_specs=(vmem, vmem),
        scratch_shapes=[
            pltpu.VMEM((wins, channels, freq), jnp.bfloat16),
            pltpu.VMEM((slots, wins, channels, freq), jnp.bfloat16),
            pltpu.VMEM((FLAG_ROWS, channels), jnp.float32),
            pltpu.VMEM((slots, FLAG_ROWS, channels), jnp.float32),
            pltpu.VMEM((128, wide), jnp.float32),
            pltpu.VMEM((2, channels, 128), jnp.float32),
            pltpu.VMEM((wins, channels, 2 * freq), jnp.bfloat16),
            pltpu.VMEM((wins, channels, 2 * freq), jnp.bfloat16),
            pltpu.VMEM((cycles, owners, own_rows, channels), jnp.bfloat16),
            pltpu.VMEM((cycles, owners - 1, own_rows, channels), jnp.bfloat16),
            pltpu.VMEM((owners, near, lanes), jnp.float32),
            pltpu.VMEM((owners - 1, near, lanes), jnp.float32),
            pltpu.SemaphoreType.DMA((wins,)),
            pltpu.SemaphoreType.DMA((slots,)),
            pltpu.SemaphoreType.DMA((slots,)),
            pltpu.SemaphoreType.DMA((slots, wins)),
            pltpu.SemaphoreType.DMA((slots, wins)),
            pltpu.SemaphoreType.DMA((cycles + 1, owners - 1)),
            pltpu.SemaphoreType.DMA((cycles + 1, owners - 1)),
        ],
        compiler_params=pltpu.CompilerParams(
            collective_id=0, has_side_effects=True, vmem_limit_bytes=48 * 1024 * 1024
        ),
        name="coherence",
    )(
        jnp.swapaxes(spectra_phase, 1, 2),
        window_valid,
        band_gain.reshape(1, freq),
        cross_index.T,
    )
    return coherence, crossing.T


def solution(mesh):
    placed = (
        P(("groups", "win"), "band", "loop"),
        P("groups", "loop"),
        P("band"),
        P(("groups", "loop"), None),
    )
    return jax.shard_map(
        on_device,
        mesh=mesh,
        in_specs=placed,
        out_specs=(
            P(("groups", "loop", "band", "win"), None, None),
            P(("groups", "loop", "band", "win"), None),
        ),
        check_vma=False,
    )
```

```python
import functools
import math

import jax
import jax.numpy as jnp
from jax import lax
from jax.experimental import pallas as pl
from jax.experimental.pallas import tpu as pltpu
from jax.sharding import PartitionSpec as P

MESH = pl.DeviceIdType.MESH
SIN = (0.9999995827674866, -0.16666549444198608, 0.008332383818924427,
       -0.00019808131037279963, 2.6991506274498533e-06, -2.033945278867577e-08)
COS = (1.0, -0.49999988079071045, 0.041666485369205475, -0.0013887780951336026,
       2.4769393348833546e-05, -2.707419355374441e-07, 1.7227314019763185e-09)
FLAG_ROWS = 8


def horner(coefficients, u):
    total = coefficients[-1] * u + coefficients[-2]
    for c in coefficients[-3::-1]:
        total = total * u + c
    return total


def cos_sin(x):
    u = x * x
    return horner(COS, u), horner(SIN, u) * x


def dot_t(a, b):
    return lax.dot_general(a, b, (((1,), (1,)), ((), ())), preferred_element_type=jnp.float32)


def row_dot(a, b):
    return lax.dot_general(a, b, (((1,), (0,)), ((), ())), preferred_element_type=jnp.float32)


def kernel(
    plan, phase_ref, valid_ref, gain_ref, index_ref, coh_ref, cross_ref,
    phase, far_phase, own_flags, far_flags, turn, columns, own_side, far_side,
    part, part_in, xpart, xpart_in,
    load_sem, flag_send, flag_recv, loop_send, loop_recv, sum_send, sum_recv,
):
    n_loop, n_band, n_win, offsets, chunk = plan
    wins, channels, freq = phase.shape
    cycles = part.shape[0]
    owners = n_band * n_win
    own_rows = channels // owners
    windows = valid_ref.shape[0]
    far_slots = len(offsets)
    loop_at = lax.axis_index("loop")
    win_at = lax.axis_index("win")
    owner_at = lax.axis_index("band") * n_win + win_at

    def loop_device(steps):
        return {"loop": lax.rem(loop_at + (steps % n_loop), n_loop)}

    def owner_of(d):
        return lax.rem(owner_at + d, owners)

    def owner_device(d):
        owner = owner_of(d)
        return {"band": owner // n_win, "win": lax.rem(owner, n_win)}

    barrier = pltpu.get_barrier_semaphore()
    greeted = sorted({o % n_loop for o in offsets} | {-o % n_loop for o in offsets})
    for steps in greeted:
        pl.semaphore_signal(barrier, inc=1, device_id=loop_device(steps), device_id_type=MESH)
    for d in range(1, owners):
        pl.semaphore_signal(barrier, inc=1, device_id=owner_device(d), device_id_type=MESH)
    loads = [
        pltpu.make_async_copy(phase_ref.at[w], phase.at[w], load_sem.at[w]) for w in range(wins)
    ]
    for load in loads:
        load.start()
    own_flags[...] = jnp.zeros_like(own_flags)
    own_flags[0:windows, :] = valid_ref[...].astype(jnp.float32)
    pl.semaphore_wait(barrier, len(greeted) + owners - 1)

    flag_copies, loop_copies = [], []
    for p, offset in enumerate(offsets):
        copy = pltpu.make_async_remote_copy(
            own_flags, far_flags.at[p], flag_send.at[p], flag_recv.at[p],
            device_id=loop_device(-offset), device_id_type=MESH,
        )
        copy.start()
        flag_copies.append(copy)
    for p, offset in enumerate(offsets):
        copies = []
        for w in range(wins):
            copy = pltpu.make_async_remote_copy(
                phase_ref.at[w], far_phase.at[p, w], loop_send.at[p, w], loop_recv.at[p, w],
                device_id=loop_device(-offset), device_id_type=MESH,
            )
            copy.start()
            copies.append(copy)
        loop_copies.append(copies)

    def window_row(flags_ref, w):
        return flags_ref[pl.ds(win_at * wins + w, 1), :]

    def turned(flags_ref, slot):
        turn[...] = jnp.zeros_like(turn)
        turn[0:FLAG_ROWS, 0:channels] = flags_ref[...]
        for w in range(wins):
            turn[FLAG_ROWS + w : FLAG_ROWS + w + 1, 0:channels] = window_row(flags_ref, w)
        columns[slot] = jnp.transpose(turn[...])[0:channels, :]

    def column(slot, w):
        return columns[slot, :, FLAG_ROWS + w : FLAG_ROWS + w + 1]

    def inverse_counts(slot, flags_ref):
        counts = row_dot(columns[slot, :, 0:FLAG_ROWS], flags_ref[...])
        return 1.0 / jnp.maximum(counts, 1.0)

    def far_trig(source, w):
        def step(c, _):
            rows = pl.ds(pl.multiple_of(c * chunk, chunk), chunk)
            cosine, sine = cos_sin(source[rows, :].astype(jnp.float32))
            far_side[w, rows, 0:freq] = cosine.astype(jnp.bfloat16)
            far_side[w, rows, freq : 2 * freq] = sine.astype(jnp.bfloat16)
            return 0

        lax.fori_loop(0, channels // chunk, step, 0)

    turned(own_flags, 0)
    gain = gain_ref[...]

    def own_trig(w):
        def step(c, _):
            rows = pl.ds(pl.multiple_of(c * chunk, chunk), chunk)
            cosine, sine = cos_sin(phase[w, rows, :].astype(jnp.float32))
            far_side[w, rows, 0:freq] = cosine.astype(jnp.bfloat16)
            far_side[w, rows, freq : 2 * freq] = sine.astype(jnp.bfloat16)
            factor = gain * columns[0, rows, FLAG_ROWS + w : FLAG_ROWS + w + 1]
            own_side[w, rows, 0:freq] = (cosine * factor).astype(jnp.bfloat16)
            own_side[w, rows, freq : 2 * freq] = (sine * factor).astype(jnp.bfloat16)
            return 0

        lax.fori_loop(0, channels // chunk, step, 0)

    sums = []

    def send_sum(piece, source, target, d):
        copy = pltpu.make_async_remote_copy(
            source.at[owner_of(d)], target.at[d - 1],
            sum_send.at[piece, d - 1], sum_recv.at[piece, d - 1],
            device_id=owner_device(d), device_id_type=MESH,
        )
        copy.start()
        sums.append(copy)

    def coherence_piece(k, flags_ref):
        ratio = dot_t(own_side[0], far_side[0]) * window_row(flags_ref, 0)
        for w in range(1, wins):
            ratio += dot_t(own_side[w], far_side[w]) * window_row(flags_ref, w)
        ratio = ratio * inverse_counts(0, flags_ref)
        for r in range(owners):
            part[k, r] = ratio[r * own_rows : (r + 1) * own_rows, :].astype(jnp.bfloat16)
        for d in range(1, owners):
            send_sum(k, part.at[k], part_in.at[k], d)

    for w in range(wins):
        loads[w].wait()
        own_trig(w)
    coherence_piece(0, own_flags)

    for p in range(far_slots):
        flags_ref = far_flags.at[p]
        flag_copies[p].wait_recv()
        if p == far_slots - 1:
            turned(flags_ref, 1)
        for w in range(wins):
            loop_copies[p][w].wait_recv()
            far_trig(far_phase.at[p, w], w)
        if p < far_slots - 1:
            coherence_piece(p + 1, flags_ref)
        else:
            ratio = dot_t(far_side[0], own_side[0]) * column(1, 0)
            for w in range(1, wins):
                ratio += dot_t(far_side[w], own_side[w]) * column(1, w)
            ratio = ratio * inverse_counts(1, own_flags)
            position = lax.broadcasted_iota(jnp.int32, ratio.shape, 0)
            near = index_ref.shape[0]
            chosen = jnp.concatenate(
                [
                    jnp.sum(
                        jnp.where(position == index_ref[n : n + 1, :], ratio, 0.0),
                        axis=0, keepdims=True,
                    )
                    for n in range(near)
                ],
                axis=0,
            )
            for r in range(owners):
                xpart[r, :, 0:own_rows] = chosen[:, r * own_rows : (r + 1) * own_rows]
            for d in range(1, owners):
                send_sum(cycles, xpart, xpart_in, d)

    for k in range(cycles):
        total = part[k, owner_at].astype(jnp.float32)
        for d in range(1, owners):
            sums[k * (owners - 1) + d - 1].wait_recv()
            total += part_in[k, d - 1].astype(jnp.float32)
        coh_ref[:, k, :] = total
    total = xpart[owner_at]
    for d in range(1, owners):
        sums[cycles * (owners - 1) + d - 1].wait_recv()
        total += xpart_in[d - 1]
    cross_ref[...] = total[:, 0:own_rows]

    for copy in flag_copies:
        copy.wait_send()
    for copies in loop_copies:
        for copy in copies:
            copy.wait_send()
    for copy in sums:
        copy.wait_send()


NEXT, OPPOSITE = 0, 1
ARRIVALS = (
    ((NEXT, 0), (NEXT, 1), (NEXT, 2), (NEXT, 3)),
    ((NEXT, 0), (NEXT, 1), (OPPOSITE, 2), (NEXT, 2), (OPPOSITE, 3), (NEXT, 3)),
    ((OPPOSITE, 0), (NEXT, 2), (OPPOSITE, 1), (NEXT, 3),
     (OPPOSITE, 2), (NEXT, 0), (OPPOSITE, 3), (NEXT, 1)),
    ((OPPOSITE, 0), (OPPOSITE, 1), (NEXT, 0), (NEXT, 1), (NEXT, 2), (NEXT, 3)),
)
OWN_SENDS = (
    ((2, OPPOSITE, 0), (2, OPPOSITE, 1), (2, OPPOSITE, 2), (2, OPPOSITE, 3)),
    ((3, OPPOSITE, 0), (0, NEXT, 0), (3, OPPOSITE, 1), (0, NEXT, 1), (0, NEXT, 2), (0, NEXT, 3)),
    ((1, NEXT, 0), (1, NEXT, 1), (1, NEXT, 2), (1, NEXT, 3)),
    ((2, NEXT, 2), (2, NEXT, 3), (2, NEXT, 0), (2, NEXT, 1)),
)
RELAYS = {
    (OPPOSITE, 0): (3, NEXT), (OPPOSITE, 1): (3, NEXT),
    (OPPOSITE, 2): (3, NEXT), (OPPOSITE, 3): (3, NEXT),
    (NEXT, 2): (1, OPPOSITE), (NEXT, 3): (1, OPPOSITE),
}
PAIR_WINDOWS = ((), (1,), (0, 1), (0,))


def kernel_of_four(
    plan, phase_ref, valid_ref, gain_ref, index_ref, coh_ref, cross_ref,
    phase, gain, index, valid, far_phase, flags, turn, columns,
    own_side, far_own, far_next, own_opposite, far_opposite, inverse,
    part, part_in, xpart, xpart_in, xopposite_in,
    load_sem, small_send, small_recv, own_send, relay_send, recv,
    sum_send, sum_recv, xsend, xrecv, ysend, yrecv,
):
    n_band, n_win, chunk = plan
    wins, channels, freq = phase.shape
    owners = n_band * n_win
    own_rows = channels // owners
    windows = valid_ref.shape[0]
    near = index_ref.shape[0]
    half = channels // 2
    at = lax.axis_index("loop")
    win_at = lax.axis_index("win")
    owner_at = lax.axis_index("band") * n_win + win_at
    across = lax.rem(at + 2, 4)
    before = lax.rem(at + 3, 4)

    def owner_of(d):
        return lax.rem(owner_at + d, owners)

    def owner_device(d, position=None):
        owner = owner_of(d)
        place = {"band": owner // n_win, "win": lax.rem(owner, n_win)}
        if position is not None:
            place["loop"] = position
        return place

    def remote(source, target, send_sem, recv_sem, device):
        return pltpu.make_async_remote_copy(
            source, target, send_sem, recv_sem, device_id=device, device_id_type=MESH
        )

    loads = [
        pltpu.make_async_copy(valid_ref, valid.at[0], load_sem.at[0]),
        pltpu.make_async_copy(gain_ref, gain, load_sem.at[1]),
        pltpu.make_async_copy(index_ref, index.at[0], load_sem.at[2]),
    ]
    for w in range(wins):
        loads.append(pltpu.make_async_copy(phase_ref.at[w], phase.at[w], load_sem.at[3 + w]))
    for load in loads:
        load.start()
    barrier = pltpu.get_barrier_semaphore()
    for steps in (1, 2, 3):
        pl.semaphore_signal(
            barrier, inc=1, device_id={"loop": lax.rem(at + steps, 4)}, device_id_type=MESH
        )
    for d in range(1, owners):
        for position in (None, across):
            pl.semaphore_signal(
                barrier, inc=1, device_id=owner_device(d, position), device_id_type=MESH
            )
    turn[...] = jnp.zeros_like(turn)
    flags[...] = jnp.zeros_like(flags)
    pl.semaphore_wait(barrier, 3 + 2 * (owners - 1))

    smalls = [
        remote(valid_ref, valid.at[1], small_send.at[0], small_recv.at[0], {"loop": before}),
        remote(valid_ref, valid.at[2], small_send.at[1], small_recv.at[1], {"loop": across}),
        remote(index_ref, index.at[1], small_send.at[2], small_recv.at[2], {"loop": across}),
    ]
    for copy in smalls:
        copy.start()

    def quarter(ref, q):
        return ref.at[q // 2, pl.ds((q % 2) * half, half)]

    def own_copies(z):
        return [
            remote(
                quarter(phase_ref, q), quarter(far_phase.at[slot], q),
                own_send.at[n], recv.at[slot, q], {"loop": target},
            )
            for n, (target, slot, q) in enumerate(OWN_SENDS[z])
        ]

    for z in range(4):
        @pl.when(at == z)
        def _():
            for copy in own_copies(z):
                copy.start()

    def window_row(slot, w):
        return flags[slot, pl.ds(win_at * wins + w, 1), :]

    def turned(flag_slot, slot):
        turn[0:FLAG_ROWS, 0:channels] = flags[flag_slot]
        for w in range(wins):
            turn[FLAG_ROWS + w : FLAG_ROWS + w + 1, 0:channels] = window_row(flag_slot, w)
        columns[slot] = jnp.transpose(turn[...])[0:channels, :]

    def column(slot, w):
        return columns[slot, :, FLAG_ROWS + w : FLAG_ROWS + w + 1]

    def inverse_counts(slot, flag_slot):
        counts = row_dot(columns[slot, :, 0:FLAG_ROWS], flags[flag_slot])
        return 1.0 / jnp.maximum(counts, 1.0)

    def trig(source, far, own, column_slot, q):
        w = q // 2
        gains = gain[...]

        def step(c, _):
            rows = pl.ds(pl.multiple_of((q % 2) * half + c * chunk, chunk), chunk)
            cosine, sine = cos_sin(source[w, rows, :].astype(jnp.float32))
            far[w, rows, 0:freq] = cosine.astype(jnp.bfloat16)
            far[w, rows, freq : 2 * freq] = sine.astype(jnp.bfloat16)
            if own is not None:
                factor = gains * columns[column_slot, rows, FLAG_ROWS + w : FLAG_ROWS + w + 1]
                own[w, rows, 0:freq] = (cosine * factor).astype(jnp.bfloat16)
                own[w, rows, freq : 2 * freq] = (sine * factor).astype(jnp.bfloat16)
            return 0

        lax.fori_loop(0, half // chunk, step, 0)

    sums = []

    def coherence_piece(k, far, scale):
        ratio = dot_t(own_side[0], far[0]) * window_row(k, 0)
        for w in range(1, wins):
            ratio += dot_t(own_side[w], far[w]) * window_row(k, w)
        ratio = ratio * scale
        for r in range(owners):
            part[k, r] = ratio[r * own_rows : (r + 1) * own_rows, :].astype(jnp.bfloat16)
        for d in range(1, owners):
            copy = remote(
                part.at[k, owner_of(d)], part_in.at[k, d - 1],
                sum_send.at[k, d - 1], sum_recv.at[k, d - 1], owner_device(d),
            )
            copy.start()
            sums.append(copy)

    def own_xcopies():
        return [
            remote(
                xpart.at[0, owner_of(d)], xpart_in.at[d - 1],
                xsend.at[d - 1], xrecv.at[d - 1], owner_device(d),
            )
            for d in range(1, owners)
        ]

    def opposite_xcopies():
        return [
            remote(
                xpart.at[1, owner_of(d)], xopposite_in.at[d],
                ysend.at[d], yrecv.at[d], owner_device(d, across),
            )
            for d in range(owners)
        ]

    def crossing_piece(side, far, own, column_slot, pair_windows):
        ratio = None
        for w in pair_windows:
            term = dot_t(far[w], own[w]) * column(column_slot, w)
            ratio = term if ratio is None else ratio + term
        ratio = ratio * inverse[1 + side]
        position = lax.broadcasted_iota(jnp.int32, ratio.shape, 0)
        rows = []
        for n in range(near):
            hit = position == index[side, n : n + 1, :]
            rows.append(jnp.sum(jnp.where(hit, ratio, 0.0), axis=0, keepdims=True))
        chosen = jnp.concatenate(rows, axis=0)
        for r in range(owners):
            xpart[side, r, :, 0:own_rows] = chosen[:, r * own_rows : (r + 1) * own_rows]

    for load in loads[:3]:
        load.wait()
    flags[0, 0:windows, :] = valid[0].astype(jnp.float32)
    turned(0, 0)
    for w in range(wins):
        loads[3 + w].wait()
        for q in (2 * w, 2 * w + 1):
            trig(phase, far_own, own_side, 0, q)
    coherence_piece(0, far_own, inverse_counts(0, 0))

    for copy in smalls:
        copy.wait_recv()
    flags[1, 0:windows, :] = valid[1].astype(jnp.float32)
    flags[2, 0:windows, :] = valid[2].astype(jnp.float32)
    turned(2, 1)
    inverse[0] = inverse_counts(0, 1)
    inverse[1] = inverse_counts(1, 0)
    inverse[2] = inverse_counts(0, 2)

    def relay_copies():
        copies = {}
        for n, ((slot, q), (target, there)) in enumerate(sorted(RELAYS.items())):
            copies[slot, q] = remote(
                quarter(far_phase.at[slot], q), quarter(far_phase.at[there], q),
                relay_send.at[n], recv.at[there, q], {"loop": target},
            )
        return copies

    for z in range(4):
        @pl.when(at == z)
        def _():
            relays = relay_copies() if z == 2 else {}
            for slot, q in ARRIVALS[z]:
                landed = quarter(far_phase.at[slot], q)
                remote(
                    landed, landed, relay_send.at[0], recv.at[slot, q], {"loop": (z + 1) % 4}
                ).wait_recv()
                if (slot, q) in relays:
                    relays[slot, q].start()
                if slot == NEXT:
                    trig(far_phase.at[NEXT], far_next, None, None, q)
                else:
                    trig(far_phase.at[OPPOSITE], far_opposite, own_opposite, 1, q)

    coherence_piece(1, far_next, inverse[0])
    for z in range(1, 4):
        @pl.when(at == z)
        def _():
            crossing_piece(1, far_own, own_opposite, 0, PAIR_WINDOWS[z])
            for copy in opposite_xcopies():
                copy.start()
            crossing_piece(0, far_opposite, own_side, 1, PAIR_WINDOWS[z])
            for copy in own_xcopies():
                copy.start()

    for k in range(2):
        total = part[k, owner_at].astype(jnp.float32)
        for d in range(1, owners):
            sums[k * (owners - 1) + d - 1].wait_recv()
            total += part_in[k, d - 1].astype(jnp.float32)
        coh_ref[:, k, :] = total

    for z in range(4):
        @pl.when(at == z)
        def _():
            total = jnp.zeros((near, xpart.shape[-1]), jnp.float32)
            if z != 0:
                total += xpart[0, owner_at]
                for d, copy in enumerate(own_xcopies()):
                    copy.wait_recv()
                    total += xpart_in[d]
            if z != 2:
                for d, copy in enumerate(opposite_xcopies()):
                    copy.wait_recv()
                    total += xopposite_in[d]
            cross_ref[...] = total[:, 0:own_rows]
            for copy in own_copies(z):
                copy.wait_send()
            if z == 2:
                for copy in relay_copies().values():
                    copy.wait_send()
            if z != 0:
                for copy in own_xcopies() + opposite_xcopies():
                    copy.wait_send()

    for copy in smalls:
        copy.wait_send()
    for copy in sums:
        copy.wait_send()


def call_of_four(phases, valid, gain, index, n_band, n_win):
    wins, channels, freq = phases.shape
    windows, near = valid.shape[0], index.shape[0]
    owners = n_band * n_win
    own_rows = channels // owners
    chunk = math.gcd(channels // 2, 32)
    lanes = -(-own_rows // 128) * 128
    wide = -(-channels // 128) * 128
    vmem = pl.BlockSpec(memory_space=pltpu.VMEM)
    hbm = pl.BlockSpec(memory_space=pltpu.HBM)
    sides = pltpu.VMEM((wins, channels, 2 * freq), jnp.bfloat16)
    dma = pltpu.SemaphoreType.DMA
    return pl.pallas_call(
        functools.partial(kernel_of_four, (n_band, n_win, chunk)),
        out_shape=(
            jax.ShapeDtypeStruct((own_rows, 2, channels), jnp.float32),
            jax.ShapeDtypeStruct((near, own_rows), jnp.float32),
        ),
        in_specs=[hbm, hbm, hbm, hbm],
        out_specs=(vmem, vmem),
        scratch_shapes=[
            pltpu.VMEM((wins, channels, freq), jnp.bfloat16),
            pltpu.VMEM((1, freq), jnp.float32),
            pltpu.VMEM((2, near, channels), jnp.int32),
            pltpu.VMEM((3, windows, channels), jnp.int32),
            pltpu.VMEM((2, wins, channels, freq), jnp.bfloat16),
            pltpu.VMEM((3, FLAG_ROWS, channels), jnp.float32),
            pltpu.VMEM((128, wide), jnp.float32),
            pltpu.VMEM((2, channels, 128), jnp.float32),
            sides, sides, sides, sides, sides,
            pltpu.VMEM((3, channels, channels), jnp.float32),
            pltpu.VMEM((2, owners, own_rows, channels), jnp.bfloat16),
            pltpu.VMEM((2, owners - 1, own_rows, channels), jnp.bfloat16),
            pltpu.VMEM((2, owners, near, lanes), jnp.float32),
            pltpu.VMEM((owners - 1, near, lanes), jnp.float32),
            pltpu.VMEM((owners, near, lanes), jnp.float32),
            dma((3 + wins,)), dma((3,)), dma((3,)), dma((6,)), dma((6,)), dma((2, 4)),
            dma((2, owners - 1)), dma((2, owners - 1)),
            dma((owners - 1,)), dma((owners - 1,)), dma((owners,)), dma((owners,)),
        ],
        compiler_params=pltpu.CompilerParams(
            collective_id=1, has_side_effects=True, vmem_limit_bytes=48 * 1024 * 1024
        ),
        name="coherence_of_four",
    )(phases, valid, gain, index)


def on_device(spectra_phase, window_valid, band_gain, cross_index):
    wins, freq, channels = spectra_phase.shape
    windows = window_valid.shape[0]
    near = cross_index.shape[1]
    n_loop = lax.axis_size("loop")
    n_band = lax.axis_size("band")
    n_win = lax.axis_size("win")
    owners = n_band * n_win
    own_rows = channels // owners
    if n_loop == 4 and wins == 2 and owners > 1:
        coherence, crossing = call_of_four(
            jnp.swapaxes(spectra_phase, 1, 2), window_valid,
            band_gain.reshape(1, freq), cross_index.T, n_band, n_win,
        )
        return coherence, crossing.T
    far_reach = n_loop // 4
    offsets = tuple(range(1, far_reach + 1)) + (n_loop // 2,)
    cycles = far_reach + 1
    slots = len(offsets)
    chunk = math.gcd(channels, 32)
    lanes = -(-own_rows // 128) * 128
    wide = -(-channels // 128) * 128
    vmem = pl.BlockSpec(memory_space=pltpu.VMEM)
    coherence, crossing = pl.pallas_call(
        functools.partial(kernel, (n_loop, n_band, n_win, offsets, chunk)),
        out_shape=(
            jax.ShapeDtypeStruct((own_rows, cycles, channels), jnp.float32),
            jax.ShapeDtypeStruct((near, own_rows), jnp.float32),
        ),
        in_specs=[pl.BlockSpec(memory_space=pl.ANY), vmem, vmem, vmem],
        out_specs=(vmem, vmem),
        scratch_shapes=[
            pltpu.VMEM((wins, channels, freq), jnp.bfloat16),
            pltpu.VMEM((slots, wins, channels, freq), jnp.bfloat16),
            pltpu.VMEM((FLAG_ROWS, channels), jnp.float32),
            pltpu.VMEM((slots, FLAG_ROWS, channels), jnp.float32),
            pltpu.VMEM((128, wide), jnp.float32),
            pltpu.VMEM((2, channels, 128), jnp.float32),
            pltpu.VMEM((wins, channels, 2 * freq), jnp.bfloat16),
            pltpu.VMEM((wins, channels, 2 * freq), jnp.bfloat16),
            pltpu.VMEM((cycles, owners, own_rows, channels), jnp.bfloat16),
            pltpu.VMEM((cycles, owners - 1, own_rows, channels), jnp.bfloat16),
            pltpu.VMEM((owners, near, lanes), jnp.float32),
            pltpu.VMEM((owners - 1, near, lanes), jnp.float32),
            pltpu.SemaphoreType.DMA((wins,)),
            pltpu.SemaphoreType.DMA((slots,)),
            pltpu.SemaphoreType.DMA((slots,)),
            pltpu.SemaphoreType.DMA((slots, wins)),
            pltpu.SemaphoreType.DMA((slots, wins)),
            pltpu.SemaphoreType.DMA((cycles + 1, owners - 1)),
            pltpu.SemaphoreType.DMA((cycles + 1, owners - 1)),
        ],
        compiler_params=pltpu.CompilerParams(
            collective_id=0, has_side_effects=True, vmem_limit_bytes=48 * 1024 * 1024
        ),
        name="coherence",
    )(
        jnp.swapaxes(spectra_phase, 1, 2),
        window_valid,
        band_gain.reshape(1, freq),
        cross_index.T,
    )
    return coherence, crossing.T


def solution(mesh):
    placed = (
        P(("groups", "win"), "band", "loop"),
        P("groups", "loop"),
        P("band"),
        P(("groups", "loop"), None),
    )
    return jax.shard_map(
        on_device,
        mesh=mesh,
        in_specs=placed,
        out_specs=(
            P(("groups", "loop", "band", "win"), None, None),
            P(("groups", "loop", "band", "win"), None),
        ),
        check_vma=False,
    )
```

```python
import functools
import math

import jax
import jax.numpy as jnp
from jax import lax
from jax.experimental import pallas as pl
from jax.experimental.pallas import tpu as pltpu
from jax.sharding import PartitionSpec as P

MESH = pl.DeviceIdType.MESH
SIN = (0.9999995827674866, -0.16666549444198608, 0.008332383818924427,
       -0.00019808131037279963, 2.6991506274498533e-06, -2.033945278867577e-08)
COS = (1.0, -0.49999988079071045, 0.041666485369205475, -0.0013887780951336026,
       2.4769393348833546e-05, -2.707419355374441e-07, 1.7227314019763185e-09)
FLAG_ROWS = 8
VMEM_OF_FOUR = 60 * 1024 * 1024


def horner(coefficients, u):
    total = coefficients[-1] * u + coefficients[-2]
    for c in coefficients[-3::-1]:
        total = total * u + c
    return total


def cos_sin(x):
    u = x * x
    return horner(COS, u), horner(SIN, u) * x


def dot_t(a, b):
    return lax.dot_general(a, b, (((1,), (1,)), ((), ())), preferred_element_type=jnp.float32)


def row_dot(a, b):
    return lax.dot_general(a, b, (((1,), (0,)), ((), ())), preferred_element_type=jnp.float32)


def kernel(
    plan, phase_ref, valid_ref, gain_ref, index_ref, coh_ref, cross_ref,
    phase, far_phase, own_flags, far_flags, turn, columns, own_side, far_side,
    part, part_in, xpart, xpart_in,
    load_sem, flag_send, flag_recv, loop_send, loop_recv, sum_send, sum_recv,
):
    n_loop, n_band, n_win, offsets, chunk = plan
    wins, channels, freq = phase.shape
    cycles = part.shape[0]
    owners = n_band * n_win
    own_rows = channels // owners
    windows = valid_ref.shape[0]
    far_slots = len(offsets)
    loop_at = lax.axis_index("loop")
    win_at = lax.axis_index("win")
    owner_at = lax.axis_index("band") * n_win + win_at

    def loop_device(steps):
        return {"loop": lax.rem(loop_at + (steps % n_loop), n_loop)}

    def owner_of(d):
        return lax.rem(owner_at + d, owners)

    def owner_device(d):
        owner = owner_of(d)
        return {"band": owner // n_win, "win": lax.rem(owner, n_win)}

    barrier = pltpu.get_barrier_semaphore()
    greeted = sorted({o % n_loop for o in offsets} | {-o % n_loop for o in offsets})
    for steps in greeted:
        pl.semaphore_signal(barrier, inc=1, device_id=loop_device(steps), device_id_type=MESH)
    for d in range(1, owners):
        pl.semaphore_signal(barrier, inc=1, device_id=owner_device(d), device_id_type=MESH)
    loads = [
        pltpu.make_async_copy(phase_ref.at[w], phase.at[w], load_sem.at[w]) for w in range(wins)
    ]
    for load in loads:
        load.start()
    own_flags[...] = jnp.zeros_like(own_flags)
    own_flags[0:windows, :] = valid_ref[...].astype(jnp.float32)
    pl.semaphore_wait(barrier, len(greeted) + owners - 1)

    flag_copies, loop_copies = [], []
    for p, offset in enumerate(offsets):
        copy = pltpu.make_async_remote_copy(
            own_flags, far_flags.at[p], flag_send.at[p], flag_recv.at[p],
            device_id=loop_device(-offset), device_id_type=MESH,
        )
        copy.start()
        flag_copies.append(copy)
    for p, offset in enumerate(offsets):
        copies = []
        for w in range(wins):
            copy = pltpu.make_async_remote_copy(
                phase_ref.at[w], far_phase.at[p, w], loop_send.at[p, w], loop_recv.at[p, w],
                device_id=loop_device(-offset), device_id_type=MESH,
            )
            copy.start()
            copies.append(copy)
        loop_copies.append(copies)

    def window_row(flags_ref, w):
        return flags_ref[pl.ds(win_at * wins + w, 1), :]

    def turned(flags_ref, slot):
        turn[...] = jnp.zeros_like(turn)
        turn[0:FLAG_ROWS, 0:channels] = flags_ref[...]
        for w in range(wins):
            turn[FLAG_ROWS + w : FLAG_ROWS + w + 1, 0:channels] = window_row(flags_ref, w)
        columns[slot] = jnp.transpose(turn[...])[0:channels, :]

    def column(slot, w):
        return columns[slot, :, FLAG_ROWS + w : FLAG_ROWS + w + 1]

    def inverse_counts(slot, flags_ref):
        counts = row_dot(columns[slot, :, 0:FLAG_ROWS], flags_ref[...])
        return 1.0 / jnp.maximum(counts, 1.0)

    def far_trig(source, w):
        def step(c, _):
            rows = pl.ds(pl.multiple_of(c * chunk, chunk), chunk)
            cosine, sine = cos_sin(source[rows, :].astype(jnp.float32))
            far_side[w, rows, 0:freq] = cosine.astype(jnp.bfloat16)
            far_side[w, rows, freq : 2 * freq] = sine.astype(jnp.bfloat16)
            return 0

        lax.fori_loop(0, channels // chunk, step, 0)

    turned(own_flags, 0)
    gain = gain_ref[...]

    def own_trig(w):
        def step(c, _):
            rows = pl.ds(pl.multiple_of(c * chunk, chunk), chunk)
            cosine, sine = cos_sin(phase[w, rows, :].astype(jnp.float32))
            far_side[w, rows, 0:freq] = cosine.astype(jnp.bfloat16)
            far_side[w, rows, freq : 2 * freq] = sine.astype(jnp.bfloat16)
            factor = gain * columns[0, rows, FLAG_ROWS + w : FLAG_ROWS + w + 1]
            own_side[w, rows, 0:freq] = (cosine * factor).astype(jnp.bfloat16)
            own_side[w, rows, freq : 2 * freq] = (sine * factor).astype(jnp.bfloat16)
            return 0

        lax.fori_loop(0, channels // chunk, step, 0)

    sums = []

    def send_sum(piece, source, target, d):
        copy = pltpu.make_async_remote_copy(
            source.at[owner_of(d)], target.at[d - 1],
            sum_send.at[piece, d - 1], sum_recv.at[piece, d - 1],
            device_id=owner_device(d), device_id_type=MESH,
        )
        copy.start()
        sums.append(copy)

    def coherence_piece(k, flags_ref):
        ratio = dot_t(own_side[0], far_side[0]) * window_row(flags_ref, 0)
        for w in range(1, wins):
            ratio += dot_t(own_side[w], far_side[w]) * window_row(flags_ref, w)
        ratio = ratio * inverse_counts(0, flags_ref)
        for r in range(owners):
            part[k, r] = ratio[r * own_rows : (r + 1) * own_rows, :].astype(jnp.bfloat16)
        for d in range(1, owners):
            send_sum(k, part.at[k], part_in.at[k], d)

    for w in range(wins):
        loads[w].wait()
        own_trig(w)
    coherence_piece(0, own_flags)

    for p in range(far_slots):
        flags_ref = far_flags.at[p]
        flag_copies[p].wait_recv()
        if p == far_slots - 1:
            turned(flags_ref, 1)
        for w in range(wins):
            loop_copies[p][w].wait_recv()
            far_trig(far_phase.at[p, w], w)
        if p < far_slots - 1:
            coherence_piece(p + 1, flags_ref)
        else:
            ratio = dot_t(far_side[0], own_side[0]) * column(1, 0)
            for w in range(1, wins):
                ratio += dot_t(far_side[w], own_side[w]) * column(1, w)
            ratio = ratio * inverse_counts(1, own_flags)
            position = lax.broadcasted_iota(jnp.int32, ratio.shape, 0)
            near = index_ref.shape[0]
            chosen = jnp.concatenate(
                [
                    jnp.sum(
                        jnp.where(position == index_ref[n : n + 1, :], ratio, 0.0),
                        axis=0, keepdims=True,
                    )
                    for n in range(near)
                ],
                axis=0,
            )
            for r in range(owners):
                xpart[r, :, 0:own_rows] = chosen[:, r * own_rows : (r + 1) * own_rows]
            for d in range(1, owners):
                send_sum(cycles, xpart, xpart_in, d)

    for k in range(cycles):
        total = part[k, owner_at].astype(jnp.float32)
        for d in range(1, owners):
            sums[k * (owners - 1) + d - 1].wait_recv()
            total += part_in[k, d - 1].astype(jnp.float32)
        coh_ref[:, k, :] = total
    total = xpart[owner_at]
    for d in range(1, owners):
        sums[cycles * (owners - 1) + d - 1].wait_recv()
        total += xpart_in[d - 1]
    cross_ref[...] = total[:, 0:own_rows]

    for copy in flag_copies:
        copy.wait_send()
    for copies in loop_copies:
        for copy in copies:
            copy.wait_send()
    for copy in sums:
        copy.wait_send()


NEXT, OPPOSITE = 0, 1
FIRST, LAST, PAIR, LATE = "first", "last", "pair", "late"
ARRIVALS = (
    ((NEXT, 0), (NEXT, 1), FIRST, (NEXT, 2), (NEXT, 3), LAST),
    ((NEXT, 0), LATE, (NEXT, 1), FIRST, (NEXT, 2), (NEXT, 3), LAST,
     (OPPOSITE, 2), (OPPOSITE, 3), PAIR),
    ((NEXT, 2), (OPPOSITE, 0), (NEXT, 3), (OPPOSITE, 1), (NEXT, 0), (NEXT, 1), FIRST,
     (OPPOSITE, 2), (OPPOSITE, 3), LAST, PAIR),
    ((NEXT, 0), (NEXT, 1), FIRST, (OPPOSITE, 0), (OPPOSITE, 1), PAIR, (NEXT, 2), (NEXT, 3), LAST),
)
OWN_SENDS = (
    ((2, OPPOSITE, 0), (2, OPPOSITE, 1), (2, OPPOSITE, 2), (2, OPPOSITE, 3)),
    ((0, NEXT, 0), (0, NEXT, 1), (0, NEXT, 2), (0, NEXT, 3), (3, OPPOSITE, 0), (3, OPPOSITE, 1)),
    ((1, NEXT, 0), (1, NEXT, 1), (1, NEXT, 2), (1, NEXT, 3)),
    ((2, NEXT, 2), (2, NEXT, 3), (2, NEXT, 0), (2, NEXT, 1)),
)
AT_ONCE = (2, 4, 4, 2)
RELAYS = {
    (OPPOSITE, 0): (3, NEXT), (OPPOSITE, 1): (3, NEXT),
    (OPPOSITE, 2): (3, NEXT), (OPPOSITE, 3): (3, NEXT),
    (NEXT, 2): (1, OPPOSITE), (NEXT, 3): (1, OPPOSITE),
}
PAIR_WINDOWS = ((), (1,), (0, 1), (0,))


def kernel_of_four(
    plan, phase_ref, valid_ref, gain_ref, index_ref, coh_ref, cross_ref,
    phase, gain, index, valid, far_phase, flags, turn, columns,
    own_side, far_own, far_next, own_opposite, far_opposite, inverse, first_term,
    part, part_in, xpart, xpart_in, xopposite_in,
    load_sem, small_send, small_recv, own_send, relay_send, recv,
    sum_send, sum_recv, xsend, xrecv, ysend, yrecv,
):
    n_band, n_win, chunk = plan
    wins, channels, freq = phase.shape
    owners = n_band * n_win
    own_rows = channels // owners
    windows = valid_ref.shape[0]
    near = index_ref.shape[0]
    half = channels // 2
    at = lax.axis_index("loop")
    win_at = lax.axis_index("win")
    owner_at = lax.axis_index("band") * n_win + win_at
    across = lax.rem(at + 2, 4)
    before = lax.rem(at + 3, 4)

    def owner_of(d):
        return lax.rem(owner_at + d, owners)

    def owner_device(d, position=None):
        owner = owner_of(d)
        place = {"band": owner // n_win, "win": lax.rem(owner, n_win)}
        if position is not None:
            place["loop"] = position
        return place

    def remote(source, target, send_sem, recv_sem, device):
        return pltpu.make_async_remote_copy(
            source, target, send_sem, recv_sem, device_id=device, device_id_type=MESH
        )

    loads = [
        pltpu.make_async_copy(valid_ref, valid.at[0], load_sem.at[0]),
        pltpu.make_async_copy(gain_ref, gain, load_sem.at[1]),
        pltpu.make_async_copy(index_ref, index.at[0], load_sem.at[2]),
    ]
    for w in range(wins):
        loads.append(pltpu.make_async_copy(phase_ref.at[w], phase.at[w], load_sem.at[3 + w]))
    for load in loads:
        load.start()
    barrier = pltpu.get_barrier_semaphore()
    for steps in (1, 2, 3):
        pl.semaphore_signal(
            barrier, inc=1, device_id={"loop": lax.rem(at + steps, 4)}, device_id_type=MESH
        )
    for d in range(1, owners):
        for position in (None, across):
            pl.semaphore_signal(
                barrier, inc=1, device_id=owner_device(d, position), device_id_type=MESH
            )
    turn[...] = jnp.zeros_like(turn)
    flags[...] = jnp.zeros_like(flags)
    pl.semaphore_wait(barrier, 3 + 2 * (owners - 1))

    smalls = [
        remote(valid_ref, valid.at[1], small_send.at[0], small_recv.at[0], {"loop": before}),
        remote(valid_ref, valid.at[2], small_send.at[1], small_recv.at[1], {"loop": across}),
        remote(index_ref, index.at[1], small_send.at[2], small_recv.at[2], {"loop": across}),
    ]
    for copy in smalls:
        copy.start()

    def quarter(ref, q):
        return ref.at[q // 2, pl.ds((q % 2) * half, half)]

    def own_copies(z):
        return [
            remote(
                quarter(phase_ref, q), quarter(far_phase.at[slot], q),
                own_send.at[n], recv.at[slot, q], {"loop": target},
            )
            for n, (target, slot, q) in enumerate(OWN_SENDS[z])
        ]

    for z in range(4):
        @pl.when(at == z)
        def _():
            for copy in own_copies(z)[: AT_ONCE[z]]:
                copy.start()

    def window_row(slot, w):
        return flags[slot, pl.ds(win_at * wins + w, 1), :]

    def turned(flag_slot, slot):
        turn[0:FLAG_ROWS, 0:channels] = flags[flag_slot]
        for w in range(wins):
            turn[FLAG_ROWS + w : FLAG_ROWS + w + 1, 0:channels] = window_row(flag_slot, w)
        columns[slot] = jnp.transpose(turn[...])[0:channels, :]

    def column(slot, w):
        return columns[slot, :, FLAG_ROWS + w : FLAG_ROWS + w + 1]

    def inverse_counts(slot, flag_slot):
        counts = row_dot(columns[slot, :, 0:FLAG_ROWS], flags[flag_slot])
        return 1.0 / jnp.maximum(counts, 1.0)

    def trig(source, far, own, column_slot, q):
        w = q // 2
        gains = gain[...]

        def step(c, _):
            rows = pl.ds(pl.multiple_of((q % 2) * half + c * chunk, chunk), chunk)
            cosine, sine = cos_sin(source[w, rows, :].astype(jnp.float32))
            far[w, rows, 0:freq] = cosine.astype(jnp.bfloat16)
            far[w, rows, freq : 2 * freq] = sine.astype(jnp.bfloat16)
            if own is not None:
                factor = gains * columns[column_slot, rows, FLAG_ROWS + w : FLAG_ROWS + w + 1]
                own[w, rows, 0:freq] = (cosine * factor).astype(jnp.bfloat16)
                own[w, rows, freq : 2 * freq] = (sine * factor).astype(jnp.bfloat16)
            return 0

        lax.fori_loop(0, half // chunk, step, 0)

    sums = []

    for k in range(2):
        for d in range(1, owners):
            sums.append(
                remote(
                    part.at[k, owner_of(d)], part_in.at[k, d - 1],
                    sum_send.at[k, d - 1], sum_recv.at[k, d - 1], owner_device(d),
                )
            )

    def window_term(k, far, w):
        return dot_t(own_side[w], far[w]) * window_row(k, w)

    def send_coherence(k, ratio):
        for r in range(owners):
            part[k, r] = ratio[r * own_rows : (r + 1) * own_rows, :].astype(jnp.bfloat16)
        for copy in sums[k * (owners - 1) : (k + 1) * (owners - 1)]:
            copy.start()

    def own_xcopies():
        return [
            remote(
                xpart.at[0, owner_of(d)], xpart_in.at[d - 1],
                xsend.at[d - 1], xrecv.at[d - 1], owner_device(d),
            )
            for d in range(1, owners)
        ]

    def opposite_xcopies():
        return [
            remote(
                xpart.at[1, owner_of(d)], xopposite_in.at[d],
                ysend.at[d], yrecv.at[d], owner_device(d, across),
            )
            for d in range(owners)
        ]

    def crossing_piece(side, far, own, column_slot, pair_windows):
        ratio = None
        for w in pair_windows:
            term = dot_t(far[w], own[w]) * column(column_slot, w)
            ratio = term if ratio is None else ratio + term
        ratio = ratio * inverse[1 + side]
        position = lax.broadcasted_iota(jnp.int32, ratio.shape, 0)
        rows = []
        for n in range(near):
            hit = position == index[side, n : n + 1, :]
            rows.append(jnp.sum(jnp.where(hit, ratio, 0.0), axis=0, keepdims=True))
        chosen = jnp.concatenate(rows, axis=0)
        for r in range(owners):
            xpart[side, r, :, 0:own_rows] = chosen[:, r * own_rows : (r + 1) * own_rows]

    for load in loads[:3]:
        load.wait()
    flags[0, 0:windows, :] = valid[0].astype(jnp.float32)
    turned(0, 0)
    for w in range(wins):
        loads[3 + w].wait()
        for q in (2 * w, 2 * w + 1):
            trig(phase, far_own, own_side, 0, q)
        for z in (0, 3):
            @pl.when(at == z)
            def _():
                copies = own_copies(z)
                copies[w].wait_send()
                copies[2 + w].start()
    own_terms = window_term(0, far_own, 0) + window_term(0, far_own, 1)
    send_coherence(0, own_terms * inverse_counts(0, 0))

    for copy in smalls:
        copy.wait_recv()
    flags[1, 0:windows, :] = valid[1].astype(jnp.float32)
    flags[2, 0:windows, :] = valid[2].astype(jnp.float32)
    turned(2, 1)
    inverse[0] = inverse_counts(0, 1)
    inverse[1] = inverse_counts(1, 0)
    inverse[2] = inverse_counts(0, 2)

    def relay_copies():
        copies = {}
        for n, ((slot, q), (target, there)) in enumerate(sorted(RELAYS.items())):
            copies[slot, q] = remote(
                quarter(far_phase.at[slot], q), quarter(far_phase.at[there], q),
                relay_send.at[n], recv.at[there, q], {"loop": target},
            )
        return copies

    for z in range(4):
        @pl.when(at == z)
        def _():
            relays = relay_copies() if z == 2 else {}
            for step in ARRIVALS[z]:
                if step == FIRST:
                    first_term[...] = window_term(1, far_next, 0)
                elif step == LAST:
                    terms = first_term[...] + window_term(1, far_next, 1)
                    send_coherence(1, terms * inverse[0])
                elif step == PAIR:
                    crossing_piece(1, far_own, own_opposite, 0, PAIR_WINDOWS[z])
                    for copy in opposite_xcopies():
                        copy.start()
                    crossing_piece(0, far_opposite, own_side, 1, PAIR_WINDOWS[z])
                    for copy in own_xcopies():
                        copy.start()
                elif step == LATE:
                    for copy in own_copies(z)[AT_ONCE[z] :]:
                        copy.start()
                else:
                    slot, q = step
                    landed = quarter(far_phase.at[slot], q)
                    remote(
                        landed, landed, relay_send.at[0], recv.at[slot, q], {"loop": (z + 1) % 4}
                    ).wait_recv()
                    if step in relays:
                        relays[step].start()
                    if slot == NEXT:
                        trig(far_phase.at[NEXT], far_next, None, None, q)
                    else:
                        trig(far_phase.at[OPPOSITE], far_opposite, own_opposite, 1, q)

    for k in range(2):
        total = part[k, owner_at].astype(jnp.float32)
        for d in range(1, owners):
            sums[k * (owners - 1) + d - 1].wait_recv()
            total += part_in[k, d - 1].astype(jnp.float32)
        coh_ref[:, k, :] = total

    for z in range(4):
        @pl.when(at == z)
        def _():
            total = jnp.zeros((near, xpart.shape[-1]), jnp.float32)
            if z != 0:
                total += xpart[0, owner_at]
                for d, copy in enumerate(own_xcopies()):
                    copy.wait_recv()
                    total += xpart_in[d]
            if z != 2:
                for d, copy in enumerate(opposite_xcopies()):
                    copy.wait_recv()
                    total += xopposite_in[d]
            cross_ref[...] = total[:, 0:own_rows]
            for copy in own_copies(z)[2 if z in (0, 3) else 0 :]:
                copy.wait_send()
            if z == 2:
                for copy in relay_copies().values():
                    copy.wait_send()
            if z != 0:
                for copy in own_xcopies() + opposite_xcopies():
                    copy.wait_send()

    for copy in smalls:
        copy.wait_send()
    for copy in sums:
        copy.wait_send()


def call_of_four(phases, valid, gain, index, n_band, n_win):
    wins, channels, freq = phases.shape
    windows, near = valid.shape[0], index.shape[0]
    owners = n_band * n_win
    own_rows = channels // owners
    chunk = math.gcd(channels // 2, 32)
    lanes = -(-own_rows // 128) * 128
    wide = -(-channels // 128) * 128
    vmem = pl.BlockSpec(memory_space=pltpu.VMEM)
    hbm = pl.BlockSpec(memory_space=pltpu.HBM)
    sides = pltpu.VMEM((wins, channels, 2 * freq), jnp.bfloat16)
    dma = pltpu.SemaphoreType.DMA
    return pl.pallas_call(
        functools.partial(kernel_of_four, (n_band, n_win, chunk)),
        out_shape=(
            jax.ShapeDtypeStruct((own_rows, 2, channels), jnp.float32),
            jax.ShapeDtypeStruct((near, own_rows), jnp.float32),
        ),
        in_specs=[hbm, hbm, hbm, hbm],
        out_specs=(vmem, vmem),
        scratch_shapes=[
            pltpu.VMEM((wins, channels, freq), jnp.bfloat16),
            pltpu.VMEM((1, freq), jnp.float32),
            pltpu.VMEM((2, near, channels), jnp.int32),
            pltpu.VMEM((3, windows, channels), jnp.int32),
            pltpu.VMEM((2, wins, channels, freq), jnp.bfloat16),
            pltpu.VMEM((3, FLAG_ROWS, channels), jnp.float32),
            pltpu.VMEM((128, wide), jnp.float32),
            pltpu.VMEM((2, channels, 128), jnp.float32),
            sides, sides, sides, sides, sides,
            pltpu.VMEM((3, channels, channels), jnp.float32),
            pltpu.VMEM((channels, channels), jnp.float32),
            pltpu.VMEM((2, owners, own_rows, channels), jnp.bfloat16),
            pltpu.VMEM((2, owners - 1, own_rows, channels), jnp.bfloat16),
            pltpu.VMEM((2, owners, near, lanes), jnp.float32),
            pltpu.VMEM((owners - 1, near, lanes), jnp.float32),
            pltpu.VMEM((owners, near, lanes), jnp.float32),
            dma((3 + wins,)), dma((3,)), dma((3,)), dma((6,)), dma((6,)), dma((2, 4)),
            dma((2, owners - 1)), dma((2, owners - 1)),
            dma((owners - 1,)), dma((owners - 1,)), dma((owners,)), dma((owners,)),
        ],
        compiler_params=pltpu.CompilerParams(
            collective_id=1, has_side_effects=True, vmem_limit_bytes=VMEM_OF_FOUR
        ),
        name="coherence_of_four",
    )(phases, valid, gain, index)


def on_device(spectra_phase, window_valid, band_gain, cross_index):
    wins, freq, channels = spectra_phase.shape
    windows = window_valid.shape[0]
    near = cross_index.shape[1]
    n_loop = lax.axis_size("loop")
    n_band = lax.axis_size("band")
    n_win = lax.axis_size("win")
    owners = n_band * n_win
    own_rows = channels // owners
    if n_loop == 4 and wins == 2 and owners > 1:
        coherence, crossing = call_of_four(
            jnp.swapaxes(spectra_phase, 1, 2), window_valid,
            band_gain.reshape(1, freq), cross_index.T, n_band, n_win,
        )
        return coherence, crossing.T
    far_reach = n_loop // 4
    offsets = tuple(range(1, far_reach + 1)) + (n_loop // 2,)
    cycles = far_reach + 1
    slots = len(offsets)
    chunk = math.gcd(channels, 32)
    lanes = -(-own_rows // 128) * 128
    wide = -(-channels // 128) * 128
    vmem = pl.BlockSpec(memory_space=pltpu.VMEM)
    coherence, crossing = pl.pallas_call(
        functools.partial(kernel, (n_loop, n_band, n_win, offsets, chunk)),
        out_shape=(
            jax.ShapeDtypeStruct((own_rows, cycles, channels), jnp.float32),
            jax.ShapeDtypeStruct((near, own_rows), jnp.float32),
        ),
        in_specs=[pl.BlockSpec(memory_space=pl.ANY), vmem, vmem, vmem],
        out_specs=(vmem, vmem),
        scratch_shapes=[
            pltpu.VMEM((wins, channels, freq), jnp.bfloat16),
            pltpu.VMEM((slots, wins, channels, freq), jnp.bfloat16),
            pltpu.VMEM((FLAG_ROWS, channels), jnp.float32),
            pltpu.VMEM((slots, FLAG_ROWS, channels), jnp.float32),
            pltpu.VMEM((128, wide), jnp.float32),
            pltpu.VMEM((2, channels, 128), jnp.float32),
            pltpu.VMEM((wins, channels, 2 * freq), jnp.bfloat16),
            pltpu.VMEM((wins, channels, 2 * freq), jnp.bfloat16),
            pltpu.VMEM((cycles, owners, own_rows, channels), jnp.bfloat16),
            pltpu.VMEM((cycles, owners - 1, own_rows, channels), jnp.bfloat16),
            pltpu.VMEM((owners, near, lanes), jnp.float32),
            pltpu.VMEM((owners - 1, near, lanes), jnp.float32),
            pltpu.SemaphoreType.DMA((wins,)),
            pltpu.SemaphoreType.DMA((slots,)),
            pltpu.SemaphoreType.DMA((slots,)),
            pltpu.SemaphoreType.DMA((slots, wins)),
            pltpu.SemaphoreType.DMA((slots, wins)),
            pltpu.SemaphoreType.DMA((cycles + 1, owners - 1)),
            pltpu.SemaphoreType.DMA((cycles + 1, owners - 1)),
        ],
        compiler_params=pltpu.CompilerParams(
            collective_id=0, has_side_effects=True, vmem_limit_bytes=48 * 1024 * 1024
        ),
        name="coherence",
    )(
        jnp.swapaxes(spectra_phase, 1, 2),
        window_valid,
        band_gain.reshape(1, freq),
        cross_index.T,
    )
    return coherence, crossing.T


def solution(mesh):
    placed = (
        P(("groups", "win"), "band", "loop"),
        P("groups", "loop"),
        P("band"),
        P(("groups", "loop"), None),
    )
    return jax.shard_map(
        on_device,
        mesh=mesh,
        in_specs=placed,
        out_specs=(
            P(("groups", "loop", "band", "win"), None, None),
            P(("groups", "loop", "band", "win"), None),
        ),
        check_vma=False,
    )
```

```python
import functools
import math

import jax
import jax.numpy as jnp
from jax import lax
from jax.experimental import pallas as pl
from jax.experimental.pallas import tpu as pltpu
from jax.sharding import PartitionSpec as P

MESH = pl.DeviceIdType.MESH
SIN = (0.9999995827674866, -0.16666549444198608, 0.008332383818924427,
       -0.00019808131037279963, 2.6991506274498533e-06, -2.033945278867577e-08)
COS = (1.0, -0.49999988079071045, 0.041666485369205475, -0.0013887780951336026,
       2.4769393348833546e-05, -2.707419355374441e-07, 1.7227314019763185e-09)
FLAG_ROWS = 8
VMEM_OF_FOUR = 60 * 1024 * 1024


def horner(coefficients, u):
    total = coefficients[-1] * u + coefficients[-2]
    for c in coefficients[-3::-1]:
        total = total * u + c
    return total


def cos_sin(x):
    u = x * x
    return horner(COS, u), horner(SIN, u) * x


def dot_t(a, b):
    return lax.dot_general(a, b, (((1,), (1,)), ((), ())), preferred_element_type=jnp.float32)


def row_dot(a, b):
    return lax.dot_general(a, b, (((1,), (0,)), ((), ())), preferred_element_type=jnp.float32)


def kernel(
    plan, phase_ref, valid_ref, gain_ref, index_ref, coh_ref, cross_ref,
    phase, far_phase, own_flags, far_flags, turn, columns, own_side, far_side,
    part, part_in, xpart, xpart_in,
    load_sem, flag_send, flag_recv, loop_send, loop_recv, sum_send, sum_recv,
):
    n_loop, n_band, n_win, offsets, chunk = plan
    wins, channels, freq = phase.shape
    cycles = part.shape[0]
    owners = n_band * n_win
    own_rows = channels // owners
    windows = valid_ref.shape[0]
    far_slots = len(offsets)
    loop_at = lax.axis_index("loop")
    win_at = lax.axis_index("win")
    owner_at = lax.axis_index("band") * n_win + win_at

    def loop_device(steps):
        return {"loop": lax.rem(loop_at + (steps % n_loop), n_loop)}

    def owner_of(d):
        return lax.rem(owner_at + d, owners)

    def owner_device(d):
        owner = owner_of(d)
        return {"band": owner // n_win, "win": lax.rem(owner, n_win)}

    barrier = pltpu.get_barrier_semaphore()
    greeted = sorted({o % n_loop for o in offsets} | {-o % n_loop for o in offsets})
    for steps in greeted:
        pl.semaphore_signal(barrier, inc=1, device_id=loop_device(steps), device_id_type=MESH)
    for d in range(1, owners):
        pl.semaphore_signal(barrier, inc=1, device_id=owner_device(d), device_id_type=MESH)
    loads = [
        pltpu.make_async_copy(phase_ref.at[w], phase.at[w], load_sem.at[w]) for w in range(wins)
    ]
    for load in loads:
        load.start()
    own_flags[...] = jnp.zeros_like(own_flags)
    own_flags[0:windows, :] = valid_ref[...].astype(jnp.float32)
    pl.semaphore_wait(barrier, len(greeted) + owners - 1)

    flag_copies, loop_copies = [], []
    for p, offset in enumerate(offsets):
        copy = pltpu.make_async_remote_copy(
            own_flags, far_flags.at[p], flag_send.at[p], flag_recv.at[p],
            device_id=loop_device(-offset), device_id_type=MESH,
        )
        copy.start()
        flag_copies.append(copy)
    for p, offset in enumerate(offsets):
        copies = []
        for w in range(wins):
            copy = pltpu.make_async_remote_copy(
                phase_ref.at[w], far_phase.at[p, w], loop_send.at[p, w], loop_recv.at[p, w],
                device_id=loop_device(-offset), device_id_type=MESH,
            )
            copy.start()
            copies.append(copy)
        loop_copies.append(copies)

    def window_row(flags_ref, w):
        return flags_ref[pl.ds(win_at * wins + w, 1), :]

    def turned(flags_ref, slot):
        turn[...] = jnp.zeros_like(turn)
        turn[0:FLAG_ROWS, 0:channels] = flags_ref[...]
        for w in range(wins):
            turn[FLAG_ROWS + w : FLAG_ROWS + w + 1, 0:channels] = window_row(flags_ref, w)
        columns[slot] = jnp.transpose(turn[...])[0:channels, :]

    def column(slot, w):
        return columns[slot, :, FLAG_ROWS + w : FLAG_ROWS + w + 1]

    def inverse_counts(slot, flags_ref):
        counts = row_dot(columns[slot, :, 0:FLAG_ROWS], flags_ref[...])
        return 1.0 / jnp.maximum(counts, 1.0)

    def far_trig(source, w):
        def step(c, _):
            rows = pl.ds(pl.multiple_of(c * chunk, chunk), chunk)
            cosine, sine = cos_sin(source[rows, :].astype(jnp.float32))
            far_side[w, rows, 0:freq] = cosine.astype(jnp.bfloat16)
            far_side[w, rows, freq : 2 * freq] = sine.astype(jnp.bfloat16)
            return 0

        lax.fori_loop(0, channels // chunk, step, 0)

    turned(own_flags, 0)
    gain = gain_ref[...]

    def own_trig(w):
        def step(c, _):
            rows = pl.ds(pl.multiple_of(c * chunk, chunk), chunk)
            cosine, sine = cos_sin(phase[w, rows, :].astype(jnp.float32))
            far_side[w, rows, 0:freq] = cosine.astype(jnp.bfloat16)
            far_side[w, rows, freq : 2 * freq] = sine.astype(jnp.bfloat16)
            factor = gain * columns[0, rows, FLAG_ROWS + w : FLAG_ROWS + w + 1]
            own_side[w, rows, 0:freq] = (cosine * factor).astype(jnp.bfloat16)
            own_side[w, rows, freq : 2 * freq] = (sine * factor).astype(jnp.bfloat16)
            return 0

        lax.fori_loop(0, channels // chunk, step, 0)

    sums = []

    def send_sum(piece, source, target, d):
        copy = pltpu.make_async_remote_copy(
            source.at[owner_of(d)], target.at[d - 1],
            sum_send.at[piece, d - 1], sum_recv.at[piece, d - 1],
            device_id=owner_device(d), device_id_type=MESH,
        )
        copy.start()
        sums.append(copy)

    def coherence_piece(k, flags_ref):
        ratio = dot_t(own_side[0], far_side[0]) * window_row(flags_ref, 0)
        for w in range(1, wins):
            ratio += dot_t(own_side[w], far_side[w]) * window_row(flags_ref, w)
        ratio = ratio * inverse_counts(0, flags_ref)
        for r in range(owners):
            part[k, r] = ratio[r * own_rows : (r + 1) * own_rows, :].astype(jnp.bfloat16)
        for d in range(1, owners):
            send_sum(k, part.at[k], part_in.at[k], d)

    for w in range(wins):
        loads[w].wait()
        own_trig(w)
    coherence_piece(0, own_flags)

    for p in range(far_slots):
        flags_ref = far_flags.at[p]
        flag_copies[p].wait_recv()
        if p == far_slots - 1:
            turned(flags_ref, 1)
        for w in range(wins):
            loop_copies[p][w].wait_recv()
            far_trig(far_phase.at[p, w], w)
        if p < far_slots - 1:
            coherence_piece(p + 1, flags_ref)
        else:
            ratio = dot_t(far_side[0], own_side[0]) * column(1, 0)
            for w in range(1, wins):
                ratio += dot_t(far_side[w], own_side[w]) * column(1, w)
            ratio = ratio * inverse_counts(1, own_flags)
            position = lax.broadcasted_iota(jnp.int32, ratio.shape, 0)
            near = index_ref.shape[0]
            chosen = jnp.concatenate(
                [
                    jnp.sum(
                        jnp.where(position == index_ref[n : n + 1, :], ratio, 0.0),
                        axis=0, keepdims=True,
                    )
                    for n in range(near)
                ],
                axis=0,
            )
            for r in range(owners):
                xpart[r, :, 0:own_rows] = chosen[:, r * own_rows : (r + 1) * own_rows]
            for d in range(1, owners):
                send_sum(cycles, xpart, xpart_in, d)

    for k in range(cycles):
        total = part[k, owner_at].astype(jnp.float32)
        for d in range(1, owners):
            sums[k * (owners - 1) + d - 1].wait_recv()
            total += part_in[k, d - 1].astype(jnp.float32)
        coh_ref[:, k, :] = total
    total = xpart[owner_at]
    for d in range(1, owners):
        sums[cycles * (owners - 1) + d - 1].wait_recv()
        total += xpart_in[d - 1]
    cross_ref[...] = total[:, 0:own_rows]

    for copy in flag_copies:
        copy.wait_send()
    for copies in loop_copies:
        for copy in copies:
            copy.wait_send()
    for copy in sums:
        copy.wait_send()


NEXT, OPPOSITE = 0, 1
FIRST, LAST, PAIR, LATE = "first", "last", "pair", "late"
ARRIVALS = (
    ((NEXT, 0), (NEXT, 1), FIRST, (NEXT, 2), (NEXT, 3), LAST),
    ((NEXT, 0), LATE, (NEXT, 1), FIRST, (NEXT, 2), (NEXT, 3), LAST,
     (OPPOSITE, 2), (OPPOSITE, 3), PAIR),
    ((OPPOSITE, 2), (OPPOSITE, 3), (OPPOSITE, 0), (OPPOSITE, 1),
     (NEXT, 0), (NEXT, 1), FIRST, (NEXT, 2), (NEXT, 3), LAST, PAIR),
    ((NEXT, 0), (NEXT, 1), FIRST, (OPPOSITE, 0), (OPPOSITE, 1), PAIR, (NEXT, 2), (NEXT, 3), LAST),
)
OWN_SENDS = (
    ((2, OPPOSITE, 0), (2, OPPOSITE, 1), (2, OPPOSITE, 2), (2, OPPOSITE, 3)),
    ((0, NEXT, 0), (0, NEXT, 1), (0, NEXT, 2), (0, NEXT, 3), (3, OPPOSITE, 0), (3, OPPOSITE, 1)),
    ((1, NEXT, 0), (1, NEXT, 1), (1, NEXT, 2), (1, NEXT, 3)),
    ((1, OPPOSITE, 2), (1, OPPOSITE, 3), (2, NEXT, 0), (2, NEXT, 1), (2, NEXT, 2), (2, NEXT, 3)),
)
AT_ONCE = (2, 4, 4, 6)
PASSED_EARLY = (0, 1)
PAIR_WINDOWS = ((), (1,), (0, 1), (0,))


def kernel_of_four(
    plan, phase_ref, valid_ref, gain_ref, index_ref, coh_ref, cross_ref,
    phase, gain, index, valid, far_phase, flags, turn, columns,
    own_side, far_own, far_next, own_opposite, far_opposite, inverse, first_term,
    part, part_in, xpart, xpart_in, xopposite_in,
    load_sem, small_send, small_recv, own_send, relay_send, recv,
    sum_send, sum_recv, xsend, xrecv, ysend, yrecv,
):
    n_band, n_win, chunk = plan
    wins, channels, freq = phase.shape
    owners = n_band * n_win
    own_rows = channels // owners
    windows = valid_ref.shape[0]
    near = index_ref.shape[0]
    half = channels // 2
    at = lax.axis_index("loop")
    win_at = lax.axis_index("win")
    owner_at = lax.axis_index("band") * n_win + win_at
    across = lax.rem(at + 2, 4)
    before = lax.rem(at + 3, 4)

    def owner_of(d):
        return lax.rem(owner_at + d, owners)

    def owner_device(d, position=None):
        owner = owner_of(d)
        place = {"band": owner // n_win, "win": lax.rem(owner, n_win)}
        if position is not None:
            place["loop"] = position
        return place

    def remote(source, target, send_sem, recv_sem, device):
        return pltpu.make_async_remote_copy(
            source, target, send_sem, recv_sem, device_id=device, device_id_type=MESH
        )

    loads = [
        pltpu.make_async_copy(valid_ref, valid.at[0], load_sem.at[0]),
        pltpu.make_async_copy(gain_ref, gain, load_sem.at[1]),
        pltpu.make_async_copy(index_ref, index.at[0], load_sem.at[2]),
    ]
    for w in range(wins):
        loads.append(pltpu.make_async_copy(phase_ref.at[w], phase.at[w], load_sem.at[3 + w]))
    for load in loads:
        load.start()
    barrier = pltpu.get_barrier_semaphore()
    for steps in (1, 2, 3):
        pl.semaphore_signal(
            barrier, inc=1, device_id={"loop": lax.rem(at + steps, 4)}, device_id_type=MESH
        )
    for d in range(1, owners):
        for position in (None, across):
            pl.semaphore_signal(
                barrier, inc=1, device_id=owner_device(d, position), device_id_type=MESH
            )
    turn[...] = jnp.zeros_like(turn)
    flags[...] = jnp.zeros_like(flags)
    pl.semaphore_wait(barrier, 3 + 2 * (owners - 1))

    smalls = [
        remote(valid_ref, valid.at[1], small_send.at[0], small_recv.at[0], {"loop": before}),
        remote(valid_ref, valid.at[2], small_send.at[1], small_recv.at[1], {"loop": across}),
        remote(index_ref, index.at[1], small_send.at[2], small_recv.at[2], {"loop": across}),
    ]
    for copy in smalls:
        copy.start()

    def quarter(ref, q):
        return ref.at[q // 2, pl.ds((q % 2) * half, half)]

    def own_copies(z):
        return [
            remote(
                quarter(phase_ref, q), quarter(far_phase.at[slot], q),
                own_send.at[n], recv.at[slot, q], {"loop": target},
            )
            for n, (target, slot, q) in enumerate(OWN_SENDS[z])
        ]

    for z in range(4):
        @pl.when(at == z)
        def _():
            for copy in own_copies(z)[: AT_ONCE[z]]:
                copy.start()

    def window_row(slot, w):
        return flags[slot, pl.ds(win_at * wins + w, 1), :]

    def turned(flag_slot, slot):
        turn[0:FLAG_ROWS, 0:channels] = flags[flag_slot]
        for w in range(wins):
            turn[FLAG_ROWS + w : FLAG_ROWS + w + 1, 0:channels] = window_row(flag_slot, w)
        columns[slot] = jnp.transpose(turn[...])[0:channels, :]

    def column(slot, w):
        return columns[slot, :, FLAG_ROWS + w : FLAG_ROWS + w + 1]

    def inverse_counts(slot, flag_slot):
        counts = row_dot(columns[slot, :, 0:FLAG_ROWS], flags[flag_slot])
        return 1.0 / jnp.maximum(counts, 1.0)

    def trig(source, far, own, column_slot, q):
        w = q // 2
        gains = gain[...]

        def step(c, _):
            rows = pl.ds(pl.multiple_of((q % 2) * half + c * chunk, chunk), chunk)
            cosine, sine = cos_sin(source[w, rows, :].astype(jnp.float32))
            far[w, rows, 0:freq] = cosine.astype(jnp.bfloat16)
            far[w, rows, freq : 2 * freq] = sine.astype(jnp.bfloat16)
            if own is not None:
                factor = gains * columns[column_slot, rows, FLAG_ROWS + w : FLAG_ROWS + w + 1]
                own[w, rows, 0:freq] = (cosine * factor).astype(jnp.bfloat16)
                own[w, rows, freq : 2 * freq] = (sine * factor).astype(jnp.bfloat16)
            return 0

        lax.fori_loop(0, half // chunk, step, 0)

    sums = []

    for k in range(2):
        for d in range(1, owners):
            sums.append(
                remote(
                    part.at[k, owner_of(d)], part_in.at[k, d - 1],
                    sum_send.at[k, d - 1], sum_recv.at[k, d - 1], owner_device(d),
                )
            )

    def window_term(k, far, w):
        return dot_t(own_side[w], far[w]) * window_row(k, w)

    def send_coherence(k, ratio):
        for r in range(owners):
            part[k, r] = ratio[r * own_rows : (r + 1) * own_rows, :].astype(jnp.bfloat16)
        for copy in sums[k * (owners - 1) : (k + 1) * (owners - 1)]:
            copy.start()

    def own_xcopies():
        return [
            remote(
                xpart.at[0, owner_of(d)], xpart_in.at[d - 1],
                xsend.at[d - 1], xrecv.at[d - 1], owner_device(d),
            )
            for d in range(1, owners)
        ]

    def opposite_xcopies():
        return [
            remote(
                xpart.at[1, owner_of(d)], xopposite_in.at[d],
                ysend.at[d], yrecv.at[d], owner_device(d, across),
            )
            for d in range(owners)
        ]

    def crossing_piece(side, far, own, column_slot, pair_windows):
        ratio = None
        for w in pair_windows:
            term = dot_t(far[w], own[w]) * column(column_slot, w)
            ratio = term if ratio is None else ratio + term
        ratio = ratio * inverse[1 + side]
        position = lax.broadcasted_iota(jnp.int32, ratio.shape, 0)
        rows = []
        for n in range(near):
            hit = position == index[side, n : n + 1, :]
            rows.append(jnp.sum(jnp.where(hit, ratio, 0.0), axis=0, keepdims=True))
        chosen = jnp.concatenate(rows, axis=0)
        for r in range(owners):
            xpart[side, r, :, 0:own_rows] = chosen[:, r * own_rows : (r + 1) * own_rows]

    for load in loads[:3]:
        load.wait()
    flags[0, 0:windows, :] = valid[0].astype(jnp.float32)
    turned(0, 0)
    for w in range(wins):
        loads[3 + w].wait()
        for q in (2 * w, 2 * w + 1):
            trig(phase, far_own, own_side, 0, q)
        @pl.when(at == 0)
        def _():
            copies = own_copies(0)
            copies[w].wait_send()
            copies[2 + w].start()

    def relay_copy(q):
        return remote(
            quarter(far_phase.at[OPPOSITE], q), quarter(far_phase.at[NEXT], q),
            relay_send.at[q], recv.at[NEXT, q], {"loop": 3},
        )

    def await_quarter(slot, q):
        landed = quarter(far_phase.at[slot], q)
        remote(
            landed, landed, relay_send.at[q], recv.at[slot, q], {"loop": lax.rem(at + 1, 4)}
        ).wait_recv()

    @pl.when(at == 2)
    def _():
        for q in PASSED_EARLY:
            await_quarter(OPPOSITE, q)
            relay_copy(q).start()

    own_terms = window_term(0, far_own, 0) + window_term(0, far_own, 1)
    send_coherence(0, own_terms * inverse_counts(0, 0))

    for copy in smalls:
        copy.wait_recv()
    flags[1, 0:windows, :] = valid[1].astype(jnp.float32)
    flags[2, 0:windows, :] = valid[2].astype(jnp.float32)
    turned(2, 1)
    inverse[0] = inverse_counts(0, 1)
    inverse[1] = inverse_counts(1, 0)
    inverse[2] = inverse_counts(0, 2)

    for z in range(4):
        @pl.when(at == z)
        def _():
            for step in ARRIVALS[z]:
                if step == FIRST:
                    first_term[...] = window_term(1, far_next, 0)
                elif step == LAST:
                    terms = first_term[...] + window_term(1, far_next, 1)
                    send_coherence(1, terms * inverse[0])
                elif step == PAIR:
                    crossing_piece(1, far_own, own_opposite, 0, PAIR_WINDOWS[z])
                    for copy in opposite_xcopies():
                        copy.start()
                    crossing_piece(0, far_opposite, own_side, 1, PAIR_WINDOWS[z])
                    for copy in own_xcopies():
                        copy.start()
                elif step == LATE:
                    for copy in own_copies(z)[AT_ONCE[z] :]:
                        copy.start()
                else:
                    slot, q = step
                    passed = z == 2 and slot == OPPOSITE
                    if not (passed and q in PASSED_EARLY):
                        await_quarter(slot, q)
                        if passed:
                            relay_copy(q).start()
                    if slot == NEXT:
                        trig(far_phase.at[NEXT], far_next, None, None, q)
                    else:
                        trig(far_phase.at[OPPOSITE], far_opposite, own_opposite, 1, q)

    for k in range(2):
        total = part[k, owner_at].astype(jnp.float32)
        for d in range(1, owners):
            sums[k * (owners - 1) + d - 1].wait_recv()
            total += part_in[k, d - 1].astype(jnp.float32)
        coh_ref[:, k, :] = total

    for z in range(4):
        @pl.when(at == z)
        def _():
            total = jnp.zeros((near, xpart.shape[-1]), jnp.float32)
            if z != 0:
                total += xpart[0, owner_at]
                for d, copy in enumerate(own_xcopies()):
                    copy.wait_recv()
                    total += xpart_in[d]
            if z != 2:
                for d, copy in enumerate(opposite_xcopies()):
                    copy.wait_recv()
                    total += xopposite_in[d]
            cross_ref[...] = total[:, 0:own_rows]
            for copy in own_copies(z)[2 if z == 0 else 0 :]:
                copy.wait_send()
            if z == 2:
                for q in range(4):
                    relay_copy(q).wait_send()
            if z != 0:
                for copy in own_xcopies() + opposite_xcopies():
                    copy.wait_send()

    for copy in smalls:
        copy.wait_send()
    for copy in sums:
        copy.wait_send()


def call_of_four(phases, valid, gain, index, n_band, n_win):
    wins, channels, freq = phases.shape
    windows, near = valid.shape[0], index.shape[0]
    owners = n_band * n_win
    own_rows = channels // owners
    chunk = math.gcd(channels // 2, 32)
    lanes = -(-own_rows // 128) * 128
    wide = -(-channels // 128) * 128
    vmem = pl.BlockSpec(memory_space=pltpu.VMEM)
    hbm = pl.BlockSpec(memory_space=pltpu.HBM)
    sides = pltpu.VMEM((wins, channels, 2 * freq), jnp.bfloat16)
    dma = pltpu.SemaphoreType.DMA
    return pl.pallas_call(
        functools.partial(kernel_of_four, (n_band, n_win, chunk)),
        out_shape=(
            jax.ShapeDtypeStruct((own_rows, 2, channels), jnp.float32),
            jax.ShapeDtypeStruct((near, own_rows), jnp.float32),
        ),
        in_specs=[hbm, hbm, hbm, hbm],
        out_specs=(vmem, vmem),
        scratch_shapes=[
            pltpu.VMEM((wins, channels, freq), jnp.bfloat16),
            pltpu.VMEM((1, freq), jnp.float32),
            pltpu.VMEM((2, near, channels), jnp.int32),
            pltpu.VMEM((3, windows, channels), jnp.int32),
            pltpu.VMEM((2, wins, channels, freq), jnp.bfloat16),
            pltpu.VMEM((3, FLAG_ROWS, channels), jnp.float32),
            pltpu.VMEM((128, wide), jnp.float32),
            pltpu.VMEM((2, channels, 128), jnp.float32),
            sides, sides, sides, sides, sides,
            pltpu.VMEM((3, channels, channels), jnp.float32),
            pltpu.VMEM((channels, channels), jnp.float32),
            pltpu.VMEM((2, owners, own_rows, channels), jnp.bfloat16),
            pltpu.VMEM((2, owners - 1, own_rows, channels), jnp.bfloat16),
            pltpu.VMEM((2, owners, near, lanes), jnp.float32),
            pltpu.VMEM((owners - 1, near, lanes), jnp.float32),
            pltpu.VMEM((owners, near, lanes), jnp.float32),
            dma((3 + wins,)), dma((3,)), dma((3,)), dma((6,)), dma((4,)), dma((2, 4)),
            dma((2, owners - 1)), dma((2, owners - 1)),
            dma((owners - 1,)), dma((owners - 1,)), dma((owners,)), dma((owners,)),
        ],
        compiler_params=pltpu.CompilerParams(
            collective_id=1, has_side_effects=True, vmem_limit_bytes=VMEM_OF_FOUR
        ),
        name="coherence_of_four",
    )(phases, valid, gain, index)


def on_device(spectra_phase, window_valid, band_gain, cross_index):
    wins, freq, channels = spectra_phase.shape
    windows = window_valid.shape[0]
    near = cross_index.shape[1]
    n_loop = lax.axis_size("loop")
    n_band = lax.axis_size("band")
    n_win = lax.axis_size("win")
    owners = n_band * n_win
    own_rows = channels // owners
    if n_loop == 4 and wins == 2 and owners > 1:
        coherence, crossing = call_of_four(
            jnp.swapaxes(spectra_phase, 1, 2), window_valid,
            band_gain.reshape(1, freq), cross_index.T, n_band, n_win,
        )
        return coherence, crossing.T
    far_reach = n_loop // 4
    offsets = tuple(range(1, far_reach + 1)) + (n_loop // 2,)
    cycles = far_reach + 1
    slots = len(offsets)
    chunk = math.gcd(channels, 32)
    lanes = -(-own_rows // 128) * 128
    wide = -(-channels // 128) * 128
    vmem = pl.BlockSpec(memory_space=pltpu.VMEM)
    coherence, crossing = pl.pallas_call(
        functools.partial(kernel, (n_loop, n_band, n_win, offsets, chunk)),
        out_shape=(
            jax.ShapeDtypeStruct((own_rows, cycles, channels), jnp.float32),
            jax.ShapeDtypeStruct((near, own_rows), jnp.float32),
        ),
        in_specs=[pl.BlockSpec(memory_space=pl.ANY), vmem, vmem, vmem],
        out_specs=(vmem, vmem),
        scratch_shapes=[
            pltpu.VMEM((wins, channels, freq), jnp.bfloat16),
            pltpu.VMEM((slots, wins, channels, freq), jnp.bfloat16),
            pltpu.VMEM((FLAG_ROWS, channels), jnp.float32),
            pltpu.VMEM((slots, FLAG_ROWS, channels), jnp.float32),
            pltpu.VMEM((128, wide), jnp.float32),
            pltpu.VMEM((2, channels, 128), jnp.float32),
            pltpu.VMEM((wins, channels, 2 * freq), jnp.bfloat16),
            pltpu.VMEM((wins, channels, 2 * freq), jnp.bfloat16),
            pltpu.VMEM((cycles, owners, own_rows, channels), jnp.bfloat16),
            pltpu.VMEM((cycles, owners - 1, own_rows, channels), jnp.bfloat16),
            pltpu.VMEM((owners, near, lanes), jnp.float32),
            pltpu.VMEM((owners - 1, near, lanes), jnp.float32),
            pltpu.SemaphoreType.DMA((wins,)),
            pltpu.SemaphoreType.DMA((slots,)),
            pltpu.SemaphoreType.DMA((slots,)),
            pltpu.SemaphoreType.DMA((slots, wins)),
            pltpu.SemaphoreType.DMA((slots, wins)),
            pltpu.SemaphoreType.DMA((cycles + 1, owners - 1)),
            pltpu.SemaphoreType.DMA((cycles + 1, owners - 1)),
        ],
        compiler_params=pltpu.CompilerParams(
            collective_id=0, has_side_effects=True, vmem_limit_bytes=48 * 1024 * 1024
        ),
        name="coherence",
    )(
        jnp.swapaxes(spectra_phase, 1, 2),
        window_valid,
        band_gain.reshape(1, freq),
        cross_index.T,
    )
    return coherence, crossing.T


def solution(mesh):
    placed = (
        P(("groups", "win"), "band", "loop"),
        P("groups", "loop"),
        P("band"),
        P(("groups", "loop"), None),
    )
    return jax.shard_map(
        on_device,
        mesh=mesh,
        in_specs=placed,
        out_specs=(
            P(("groups", "loop", "band", "win"), None, None),
            P(("groups", "loop", "band", "win"), None),
        ),
        check_vma=False,
    )
```
